32 devices in a mesh: col: 32 (over z, y, x, core).
Axes of the slice: x: 2, y: 2, z: 4, core: 2. Of those that a mesh axis runs over, the one named last changes fastest.
Arguments:
- final_adjoint: float32 [7, 50, 4096], P(None, None, 'col'), may hold values from -6 to 6
- states: float32 [3, 7, 50, 4096], P(None, None, None, 'col'), may hold values from 0.05 to 3
- implicit: float32 [50, 50, 4096], P(None, None, 'col'), may hold values from -0.6 to 1
- wet_levels: int32 [4096], P('col'), may hold values from 12 to 50
- tile_rows: int32 [960], P('col'), may hold values from 0 to 1599, as said below
- tile_cols: int32 [960], P('col'), may hold values from 0 to 1599, as said below
- tiles: bfloat16 [960, 128, 128], P('col'), may hold values from -0.3984375 to 0.3984375
- tile_count: int32 [32], P('col'), may hold values from 5 to 30, as said below
Outputs:
- initial_adjoint: float32 [7, 50, 4096], P(None, None, 'col')
The draws below stay inside these ranges and needn't reach their ends.
Inputs may be any that keep to these rules, and one draw needn't show every extreme that they name: `tile_rows`: a tile slot of device d names a row block of device d. `tile_cols`: a tile's column block lies on a device at most 2 away from the device of its row block. Slots from tile_count on are not part of the matrix; some device fills all 30 slots.
All inputs are finite; a program needn't handle non-finite values.
Results may differ from the reference program's by a relative error of at most 0.0003.
Values sent between devices are 32-bit elements; how exact they have to be, the bound alone decides.
A program may use at most 64 MiB of HBM per device.

```python
import math
import jax
import jax.numpy as jnp
from jax import lax

TRC = 7
LEV = 50
COL_DEV = 128
STEPS = 3
REACH = 2
BLOCKS_DEV = 50
TILE_MAX = 30
BLOCKS = 1600
COLUMNS = 4096
N_COL = 32


def draw_implicit(key, part):
    key = jax.random.fold_in(key, 5)
    first, second = jax.random.split(key)
    diagonal = 0.6 + 0.3 * jax.random.uniform(first, (1, LEV, COLUMNS), jnp.float32)
    spread = jnp.clip(0.35 * jax.random.normal(second, (LEV, LEV, COLUMNS), jnp.float32), -0.6, 0.6) / LEV ** 0.5
    upper = jax.lax.broadcasted_iota(jnp.int32, (LEV, LEV, COLUMNS), 0)
    lower = jax.lax.broadcasted_iota(jnp.int32, (LEV, LEV, COLUMNS), 1)
    return jnp.where(upper == lower, diagonal, spread).astype(jnp.float32)


def draw_wet_levels(key, part):
    key = jax.random.fold_in(key, 7)
    levels = jax.random.randint(key, (COLUMNS,), LEV // 4, LEV + 1)
    return levels.at[0].set(LEV).at[1].set(LEV // 4).astype(jnp.int32)


def draw_tile_rows(key, part):
    key = jax.random.fold_in(key, 11)
    owner = jnp.arange(TILE_MAX * N_COL, dtype=jnp.int32) // TILE_MAX
    local = jax.random.randint(key, (TILE_MAX * N_COL,), 0, BLOCKS_DEV)
    rows = owner * BLOCKS_DEV + local
    return rows.at[0].set(0).at[TILE_MAX * N_COL - 1].set(BLOCKS - 1).astype(jnp.int32)


def draw_tile_cols(key, part):
    key = jax.random.fold_in(key, 13)
    first, second = jax.random.split(key)
    position = jnp.arange(TILE_MAX * N_COL, dtype=jnp.int32)
    owner = position // TILE_MAX
    within = position % TILE_MAX
    drawn = jax.random.randint(first, (TILE_MAX * N_COL,), -REACH, REACH + 1)
    offset = jnp.where(within < 2 * REACH + 1, within - REACH, drawn)
    target = jnp.clip(owner + offset, 0, N_COL - 1)
    local = jax.random.randint(second, (TILE_MAX * N_COL,), 0, BLOCKS_DEV)
    cols = target * BLOCKS_DEV + local
    return cols.at[0].set(0).at[TILE_MAX * N_COL - 1].set(BLOCKS - 1).astype(jnp.int32)


def draw_tile_count(key, part):
    key = jax.random.fold_in(key, 17)
    first, second, third = jax.random.split(key, 3)
    lowest = 2 * REACH + 1
    base = jax.random.randint(first, (N_COL,), lowest, TILE_MAX)
    filled = jax.random.randint(second, (N_COL,), 0, 8) == 0
    chosen = jax.random.randint(third, (), 0, N_COL)
    filled = filled | (jnp.arange(N_COL, dtype=jnp.int32) == chosen)
    return jnp.where(filled, TILE_MAX, base).astype(jnp.int32)


def level_of(stream_key, extent, pieces, smallest, top_value):
    gain, own = 1.0, jax.random.fold_in(stream_key, 6)
    for dim, blocks in pieces:
        heights = jnp.exp(jax.random.uniform(jax.random.fold_in(own, dim), (blocks,), jnp.float32, smallest / len(pieces), top_value / len(pieces)))
        gain = gain * jnp.repeat(heights, extent[dim] // blocks).reshape([-1 if axis == dim else 1 for axis in range(len(extent))])
    return gain


def noise(stream_key, extent, deviation, limit, cuts=(), held_as=jnp.bfloat16):
    array = jax.random.normal(stream_key, extent, jnp.float32) * deviation
    if len(cuts) > 0:
        array = level_of(stream_key, extent, cuts, -0.22, 0.18) * array
    return jnp.clip(array, min=-limit, max=limit).astype(held_as)


def setup_inputs(seed: int = 0) -> dict:
    keys = jax.random.split(jax.random.key(seed), 9)
    return {
        "final_adjoint": noise(keys[0], (TRC, LEV, COLUMNS), 1.0, 6.0, ((2, 32),), jnp.float32),
        "states": jnp.clip(jnp.exp(math.log(3.0) - 4.0943445 * jax.random.uniform(keys[1], (STEPS, TRC, LEV, COLUMNS), jnp.float32) ** level_of(keys[1], (STEPS, TRC, LEV, COLUMNS), ((3, 32),), -0.2, 0.2)), 0.05, 3.0),
        "implicit": draw_implicit(jax.random.fold_in(keys[8], 71), 0),
        "wet_levels": draw_wet_levels(jax.random.fold_in(keys[8], 71), 0),
        "tile_rows": draw_tile_rows(jax.random.fold_in(keys[8], 71), 0),
        "tile_cols": draw_tile_cols(jax.random.fold_in(keys[8], 71), 0),
        "tiles": noise(keys[6], (TILE_MAX * N_COL, 128, 128), 0.05, 0.3984375, ((0, 32),)),
        "tile_count": draw_tile_count(jax.random.fold_in(keys[8], 71), 0),
    }


def sources(state, light_factor):
    phosphate, dissolved, oxygen, plankton, grazers, detritus, nitrate = [state[i] for i in range(7)]
    growth = 1.2 * light_factor * plankton * phosphate / (0.03 + phosphate) * nitrate / (0.5 + nitrate)
    grazing = 1.9 * grazers * plankton * plankton / (0.1 + plankton * plankton)
    mortality = 0.03 * plankton * plankton
    remineral = 0.05 * detritus * oxygen / (1.0 + oxygen)
    dop_decay = 0.17 * dissolved
    grazer_loss = 0.05 * grazers * grazers
    return jnp.stack([-growth + remineral + dop_decay + 0.3 * grazing, 0.1 * growth + 0.1 * mortality - dop_decay, 1.2 * (growth - remineral - dop_decay), growth - grazing - mortality, 0.7 * grazing - grazer_loss, grazer_loss + 0.9 * mortality - remineral, 1.6 * (remineral + dop_decay - growth)])

def to_blocks(field):
    shaped = field.reshape(TRC, LEV, N_COL, COL_DEV // 128, 128)
    return jnp.transpose(shaped, (2, 1, 3, 0, 4)).reshape(BLOCKS, TRC, 128)

def from_blocks(blocked):
    shaped = blocked.reshape(N_COL, LEV, COL_DEV // 128, TRC, 128)
    return jnp.transpose(shaped, (3, 1, 0, 2, 4)).reshape(TRC, LEV, COLUMNS)

def reference(final_adjoint, states, implicit, wet_levels, tile_rows, tile_cols, tiles, tile_count):
    levels = lax.broadcasted_iota(jnp.int32, (LEV, COLUMNS), 0)
    wet_mask = (levels < wet_levels[None, :]).astype(jnp.float32)
    light_factor = jnp.exp(-0.2 * lax.broadcasted_iota(jnp.int32, (LEV, 1), 0).astype(jnp.float32))
    row_table = tile_rows.reshape(N_COL, TILE_MAX)
    tile_table = tiles.reshape(N_COL, TILE_MAX, 128, 128)
    active = (lax.broadcasted_iota(jnp.int32, (N_COL, TILE_MAX), 1) < tile_count[:, None]).astype(jnp.float32)
    adjoint = final_adjoint
    for section in range(STEPS - 1, -1, -1):
        carried = jnp.einsum('klc,tkc->tlc', implicit, adjoint, precision=lax.Precision.HIGHEST) * wet_mask
        blocked = to_blocks(carried)

        def device_terms(packed):
            row_ids, matrices, weights = packed
            picked = blocked[row_ids]
            terms = jnp.einsum('sci,sij->scj', picked, matrices.astype(jnp.float32), precision=lax.Precision.HIGHEST)
            return terms * weights[:, None, None]
        contributions = lax.map(device_terms, (row_table, tile_table, active))
        summed = jax.ops.segment_sum(contributions.reshape(-1, TRC, 128), tile_cols, num_segments=BLOCKS)
        transport = from_blocks(summed)
        unused, pull_back = jax.vjp(lambda state: sources(state, light_factor), states[section])
        biology = pull_back(carried)[0]
        adjoint = wet_mask * (carried + transport + 0.5 * biology)
    return adjoint
```

```python
import functools

import jax
import jax.numpy as jnp
from jax import lax
from jax.experimental import pallas as pl
from jax.experimental.pallas import tpu as pltpu
from jax.sharding import PartitionSpec as P

STEPS = 3
REACH = 2
OFFSETS = (-2, 2, -1, 1)
TIME_STEP = 0.5


def biology(c, s, light):
    phosphate, _, oxygen, plankton, grazers, detritus, nitrate = s
    inv_p = 1.0 / (0.03 + phosphate)
    inv_n = 1.0 / (0.5 + nitrate)
    inv_o = 1.0 / (1.0 + oxygen)
    square = plankton * plankton
    inv_z = 1.0 / (0.1 + square)
    up = phosphate * inv_p
    un = nitrate * inv_n
    c_growth = -c[0] + 0.1 * c[1] + 1.2 * c[2] + c[3] - 1.6 * c[6]
    c_grazing = 0.3 * c[0] - c[3] + 0.7 * c[4]
    c_mortality = 0.1 * c[1] - c[3] + 0.9 * c[5]
    c_remineral = c[0] - 1.2 * c[2] - c[5] + 1.6 * c[6]
    c_decay = c[0] - c[1] - 1.2 * c[2] + 1.6 * c[6]
    c_loss = c[5] - c[4]
    g = c_growth * (1.2 * light)
    gz = g * plankton
    q = 0.05 * c_remineral
    return (
        gz * un * (0.03 * inv_p * inv_p),
        0.17 * c_decay,
        q * detritus * (inv_o * inv_o),
        g * up * un
        + c_grazing * grazers * plankton * (0.38 * inv_z * inv_z)
        + 0.06 * c_mortality * plankton,
        1.9 * c_grazing * square * inv_z + 0.1 * c_loss * grazers,
        q * oxygen * inv_o,
        gz * up * (0.5 * inv_n * inv_n),
    )


def split(x):
    hi = x.astype(jnp.bfloat16)
    lo = (x - hi.astype(jnp.float32)).astype(jnp.bfloat16)
    return hi, lo


def kernel(
    peers, slots, slots_pad, blocks,
    adj_hbm, states_hbm, imp_hbm, wet_ref, rows_ref, cols_ref, tiles_hbm, count_ref,
    out_ref,
    adj, states, imp, tiles, carried, by_block, sent, got, ids, got_ids,
    load_sem, id_send, id_recv, send_sem, recv_sem,
):
    tracers, levels, width = adj.shape
    body = tracers * slots_pad
    by_row = by_block.reshape(blocks * 8, 128)
    me = lax.axis_index("col")

    loads = [
        pltpu.make_async_copy(src, dst, load_sem.at[i])
        for i, (src, dst) in enumerate(
            ((adj_hbm, adj), (imp_hbm, imp), (tiles_hbm, tiles), (states_hbm, states))
        )
    ]
    for load in loads:
        load.start()

    inside = [(me + off >= 0) & (me + off < peers) for off in OFFSETS]

    barrier = pltpu.get_barrier_semaphore()
    for off, ok in zip(OFFSETS, inside):
        @pl.when(ok)
        def _():
            pl.semaphore_signal(
                barrier, inc=1, device_id=(me + off,), device_id_type=pl.DeviceIdType.MESH
            )

    lane_slot = lax.broadcasted_iota(jnp.int32, (8, 128), 1) % slots_pad
    own_ids = jnp.full((8, 128), -1, jnp.int32)
    for s in range(slots):
        own_ids = jnp.where(lane_slot == s, cols_ref[s], own_ids)
    own_ids = jnp.where(lane_slot < count_ref[0], own_ids, -1)
    ids[...] = own_ids
    zero_row = jnp.zeros((8, 128), jnp.float32)
    for n in range(STEPS):
        for s in range(slots, slots_pad):
            sent[n, pl.ds(s, 8, stride=slots_pad), :] = zero_row
    for first in range(0, levels, 8):
        rows = min(8, levels - first)
        by_row[pl.ds(first * 8 + 7, rows, stride=8), :] = jnp.zeros((rows, 128), jnp.float32)

    for i, ok in enumerate(inside):
        @pl.when(jnp.logical_not(ok))
        def _():
            got_ids[i] = jnp.full((8, 128), -1, jnp.int32)
            for n in range(STEPS):
                got[n, i] = jnp.zeros((body, 128), jnp.float32)

    pl.semaphore_wait(barrier, sum(ok.astype(jnp.int32) for ok in inside))

    def place_of(off):
        return OFFSETS.index(-off)

    id_copies = [
        pltpu.make_async_remote_copy(
            src_ref=ids, dst_ref=got_ids.at[place_of(off)],
            send_sem=id_send.at[i], recv_sem=id_recv.at[place_of(off)],
            device_id=(me + off,), device_id_type=pl.DeviceIdType.MESH,
        )
        for i, off in enumerate(OFFSETS)
    ]
    for copy, ok in zip(id_copies, inside):
        pl.when(ok)(copy.start)

    level = lax.broadcasted_iota(jnp.int32, (levels, width), 0)

    def wet(first, rows):
        ids_ = lax.broadcasted_iota(jnp.int32, (rows, width), 0) + first
        return (ids_ < wet_ref[...]).astype(jnp.float32)

    loads[0].wait()
    loads[1].wait()

    block_row = lax.broadcasted_iota(jnp.int32, (blocks, 2 * slots_pad), 0)
    own_pick = (block_row == own_ids[0:1, : 2 * slots_pad] - me * blocks).astype(jnp.bfloat16)
    near_pick = None

    for n in range(STEPS):
        section = STEPS - 1 - n
        for first in range(0, levels, 32):
            rows = min(32, levels - first)
            acc = [None] * tracers
            for k in range(levels):
                m = imp[k, pl.ds(first, rows), :]
                for t in range(tracers):
                    term = m * adj[t, pl.ds(k, 1), :]
                    acc[t] = term if acc[t] is None else acc[t] + term
            mask = wet(first, rows)
            for t in range(tracers):
                value = acc[t] * mask
                carried[t, pl.ds(first, rows), :] = value
                for r in range(0, rows, 8):
                    some = min(8, rows - r)
                    by_row[pl.ds((first + r) * 8 + t, some, stride=8), :] = value[r : r + some]
        if n == 0:
            loads[2].wait()
        for s in range(slots):
            row = jnp.minimum(jnp.maximum(rows_ref[s] - me * blocks, 0), blocks - 1)
            hi, lo = split(by_block[row])
            term = jnp.dot(
                jnp.concatenate([hi, lo], axis=0), tiles[s], preferred_element_type=jnp.float32
            )
            sent[n, pl.ds(s, 8, stride=slots_pad), :] = term[:8] + term[8:]
        copies = [
            pltpu.make_async_remote_copy(
                src_ref=sent.at[n, pl.ds(0, body)], dst_ref=got.at[n, place_of(off)],
                send_sem=send_sem.at[n, i], recv_sem=recv_sem.at[n, place_of(off)],
                device_id=(me + off,), device_id_type=pl.DeviceIdType.MESH,
            )
            for i, off in enumerate(OFFSETS)
        ]
        for copy, ok in zip(copies, inside):
            pl.when(ok)(copy.start)

        if n == 0:
            loads[3].wait()
        own = []
        for t in range(tracers):
            hi, lo = split(sent[n, pl.ds(t * slots_pad, slots_pad), :])
            own.append(jnp.concatenate([hi, lo], axis=0))
        own_sum = jnp.dot(
            own_pick, jnp.concatenate(own, axis=1), preferred_element_type=jnp.float32
        )
        for first in range(0, levels, 8):
            rows = min(8, levels - first)
            part = pl.ds(first, rows)
            mask = wet(first, rows)
            depth = (lax.broadcasted_iota(jnp.int32, (rows, width), 0) + first).astype(jnp.float32)
            light = jnp.exp(-0.2 * depth)
            c = [carried[t, part, :] for t in range(tracers)]
            state = [states[section, t, part, :] for t in range(tracers)]
            bio = biology(c, state, light)
            for t in range(tracers):
                own_part = own_sum[first : first + rows, t * 128 : (t + 1) * 128]
                adj[t, part, :] = mask * (c[t] + own_part + TIME_STEP * bio[t])

        if n == 0:
            for i, off in enumerate(OFFSETS):
                pl.when(inside[i])(id_copies[place_of(off)].wait_recv)
            lanes = lax.broadcasted_iota(jnp.int32, (8, 128), 1) // slots_pad
            near = got_ids[0]
            for i in range(1, len(OFFSETS)):
                near = jnp.where(lanes == i, got_ids[i], near)
            rows_near = lax.broadcasted_iota(jnp.int32, (blocks, 128), 0)
            near_pick = (rows_near == near[0:1] - me * blocks).astype(jnp.bfloat16)
            near_pick = jnp.concatenate([near_pick, near_pick], axis=1)
        for i in range(len(OFFSETS)):
            pl.when(inside[i])(copies[place_of(OFFSETS[i])].wait_recv)
        near_terms = []
        for t in range(tracers):
            pieces = [got[n, i, pl.ds(t * slots_pad, slots_pad), :] for i in range(len(OFFSETS))]
            hi, lo = split(jnp.concatenate(pieces, axis=0))
            near_terms.append(jnp.concatenate([hi, lo], axis=0))
        near_sum = jnp.dot(
            near_pick, jnp.concatenate(near_terms, axis=1), preferred_element_type=jnp.float32
        )
        mask = wet(0, levels)
        for t in range(tracers):
            value = adj[t] + mask * near_sum[:, t * 128 : (t + 1) * 128]
            if n == STEPS - 1:
                out_ref[t] = value
            else:
                adj[t] = value
        for copy, ok in zip(copies, inside):
            pl.when(ok)(copy.wait_send)
    for copy, ok in zip(id_copies, inside):
        pl.when(ok)(copy.wait_send)


def shards(peers, final_adjoint, states, implicit, wet_levels, tile_rows, tile_cols, tiles, tile_count):
    tracers, levels, width = final_adjoint.shape
    blocks = levels * width // 128
    slots = tiles.shape[0]
    slots_pad = -(-slots // 32) * 32
    body = tracers * slots_pad
    near = len(OFFSETS)
    hbm = pl.BlockSpec(memory_space=pl.ANY)
    smem = pl.BlockSpec(memory_space=pltpu.SMEM)
    vmem = pl.BlockSpec(memory_space=pltpu.VMEM)
    f32 = jnp.float32
    return pl.pallas_call(
        functools.partial(kernel, peers, slots, slots_pad, blocks),
        out_shape=jax.ShapeDtypeStruct((tracers, levels, width), f32),
        in_specs=[hbm, hbm, hbm, vmem, smem, smem, hbm, smem],
        out_specs=vmem,
        scratch_shapes=[
            pltpu.VMEM((tracers, levels, width), f32),
            pltpu.VMEM(states.shape, f32),
            pltpu.VMEM(implicit.shape, f32),
            pltpu.VMEM(tiles.shape, tiles.dtype),
            pltpu.VMEM((tracers, levels, width), f32),
            pltpu.VMEM((blocks, 8, 128), f32),
            pltpu.VMEM((STEPS, 8 * slots_pad, 128), f32),
            pltpu.VMEM((STEPS, near, body, 128), f32),
            pltpu.VMEM((8, 128), jnp.int32),
            pltpu.VMEM((near, 8, 128), jnp.int32),
            pltpu.SemaphoreType.DMA((4,)),
            pltpu.SemaphoreType.DMA((near,)),
            pltpu.SemaphoreType.DMA((near,)),
            pltpu.SemaphoreType.DMA((STEPS, near)),
            pltpu.SemaphoreType.DMA((STEPS, near)),
        ],
        compiler_params=pltpu.CompilerParams(
            collective_id=0, has_side_effects=True, vmem_limit_bytes=32 * 1024 * 1024
        ),
    )(
        final_adjoint, states, implicit, wet_levels.reshape(1, width),
        tile_rows, tile_cols, tiles, tile_count,
    )


def solution(mesh):
    in_specs = (
        P(None, None, "col"),
        P(None, None, None, "col"),
        P(None, None, "col"),
        P("col"),
        P("col"),
        P("col"),
        P("col", None, None),
        P("col"),
    )
    out_specs = P(None, None, "col")
    return jax.shard_map(
        functools.partial(shards, mesh.shape["col"]),
        mesh=mesh, in_specs=in_specs, out_specs=out_specs, check_vma=False,
    )
```

```python
import functools

import jax
import jax.numpy as jnp
from jax import lax
from jax.experimental import pallas as pl
from jax.experimental.pallas import tpu as pltpu
from jax.sharding import PartitionSpec as P

STEPS = 3
REACH = 2
CHUNK = 8
PARTNER, ACROSS, RELAYED, PASSED = range(4)
TIME_STEP = 0.5


def biology(c, s, light):
    phosphate, _, oxygen, plankton, grazers, detritus, nitrate = s
    inv_p = 1.0 / (0.03 + phosphate)
    inv_n = 1.0 / (0.5 + nitrate)
    inv_o = 1.0 / (1.0 + oxygen)
    square = plankton * plankton
    inv_z = 1.0 / (0.1 + square)
    up = phosphate * inv_p
    un = nitrate * inv_n
    c_growth = -c[0] + 0.1 * c[1] + 1.2 * c[2] + c[3] - 1.6 * c[6]
    c_grazing = 0.3 * c[0] - c[3] + 0.7 * c[4]
    c_mortality = 0.1 * c[1] - c[3] + 0.9 * c[5]
    c_remineral = c[0] - 1.2 * c[2] - c[5] + 1.6 * c[6]
    c_decay = c[0] - c[1] - 1.2 * c[2] + 1.6 * c[6]
    c_loss = c[5] - c[4]
    g = c_growth * (1.2 * light)
    gz = g * plankton
    q = 0.05 * c_remineral
    return (
        gz * un * (0.03 * inv_p * inv_p),
        0.17 * c_decay,
        q * detritus * (inv_o * inv_o),
        g * up * un
        + c_grazing * grazers * plankton * (0.38 * inv_z * inv_z)
        + 0.06 * c_mortality * plankton,
        1.9 * c_grazing * square * inv_z + 0.1 * c_loss * grazers,
        q * oxygen * inv_o,
        gz * up * (0.5 * inv_n * inv_n),
    )


def split(x):
    hi = x.astype(jnp.bfloat16)
    lo = (x - hi.astype(jnp.float32)).astype(jnp.bfloat16)
    return hi, lo


def kernel(
    peers, slots, chunks, blocks,
    adj_hbm, states_hbm, imp_hbm, wet_ref, rows_ref, cols_ref, tiles_hbm, count_ref,
    out_ref,
    adj, states, imp, tiles, carried, by_block, sent, got,
    load_sem, send_sem, recv_sem,
):
    tracers, levels, width = adj.shape
    slots_pad = chunks * CHUNK
    body = tracers * CHUNK
    by_row = by_block.reshape(blocks * 8, 128)
    me = lax.axis_index("col")
    chip = me // 2
    core = me % 2
    odd = chip % 2
    partner = me + 1 - 2 * core
    across = me + 2 - 4 * odd
    relay_to = me + 4 - 8 * odd
    relay_from = me - 4 + 8 * odd
    relays = (relay_to >= 0) & (relay_to < peers)
    relayed = (relay_from >= 0) & (relay_from < peers)
    passes_across = core == odd
    passes_relayed = (core != odd) & relayed
    gets_passed = (core != odd) | relayed
    misses_passed = (core == odd) & jnp.logical_not(relayed)

    loads = [
        pltpu.make_async_copy(src, dst, load_sem.at[i])
        for i, (src, dst) in enumerate(
            ((adj_hbm, adj), (imp_hbm, imp), (tiles_hbm, tiles), (states_hbm, states))
        )
    ]
    for load in loads:
        load.start()

    barrier = pltpu.get_barrier_semaphore()

    def greet(device):
        pl.semaphore_signal(
            barrier, inc=1, device_id=(device,), device_id_type=pl.DeviceIdType.MESH
        )

    greet(partner)
    greet(across)
    pl.when(relays)(lambda: greet(relay_to))
    pl.when(relayed)(lambda: greet(relay_from))

    lane = lax.broadcasted_iota(jnp.int32, (8, 128), 1)
    lane_slot = lane % slots_pad
    own_ids = jnp.full((8, 128), -1, jnp.int32)
    for s in range(slots):
        own_ids = jnp.where(lane_slot == s, cols_ref[s], own_ids)
    own_ids = jnp.where(lane_slot < count_ref[0], own_ids, -1).astype(jnp.float32)
    zero_tile = jnp.zeros((8, 128), jnp.float32)
    for n in range(STEPS):
        for s in range(slots, slots_pad):
            sent[n, s // CHUNK, pl.ds(s % CHUNK, 8, stride=CHUNK), :] = zero_tile
    for first in range(0, levels, 8):
        rows = min(8, levels - first)
        by_row[pl.ds(first * 8 + 7, rows, stride=8), :] = jnp.zeros((rows, 128), jnp.float32)

    def blank(place):
        for n in range(STEPS):
            for q in range(chunks):
                got[n, place, q] = jnp.zeros(got.shape[3:], jnp.float32)
        got[0, place, 0, pl.ds(body, 8), :] = jnp.full((8, 128), -1.0, jnp.float32)

    pl.when(jnp.logical_not(relayed))(lambda: blank(RELAYED))
    pl.when(misses_passed)(lambda: blank(PASSED))

    pl.semaphore_wait(
        barrier, 2 + relays.astype(jnp.int32) + relayed.astype(jnp.int32)
    )

    def copy_of(n, q, source, place, device):
        size = body + (8 if n == 0 and q == 0 else 0)
        return pltpu.make_async_remote_copy(
            src_ref=source.at[pl.ds(0, size)], dst_ref=got.at[n, place, q, pl.ds(0, size)],
            send_sem=send_sem.at[n, place, q], recv_sem=recv_sem.at[n, place, q],
            device_id=(device,), device_id_type=pl.DeviceIdType.MESH,
        )

    def wet(first, rows):
        level = lax.broadcasted_iota(jnp.int32, (rows, width), 0) + first
        return (level < wet_ref[...]).astype(jnp.float32)

    def pick_of(targets):
        block = lax.broadcasted_iota(jnp.int32, (blocks, targets.shape[1]), 0) + me * blocks
        pick = (block.astype(jnp.float32) == targets).astype(jnp.bfloat16)
        return jnp.concatenate([pick, pick], axis=1)

    def placed(pick, sources):
        columns = []
        for t in range(tracers):
            pieces = [ref[q, pl.ds(t * CHUNK, CHUNK), :] for ref in sources for q in range(chunks)]
            columns.append(jnp.concatenate(split(jnp.concatenate(pieces, axis=0)), axis=0))
        return jnp.dot(pick, jnp.concatenate(columns, axis=1), preferred_element_type=jnp.float32)

    loads[0].wait()
    loads[1].wait()
    own_pick = pick_of(own_ids[0:1, :slots_pad])
    near_pick = far_pick = None
    level_parts = [(first, min(8, levels - first)) for first in range(0, levels, 8)]
    per_chunk = -(-len(level_parts) // chunks)
    started = []

    for n in range(STEPS):
        section = STEPS - 1 - n
        for first in range(0, levels, 32):
            rows = min(32, levels - first)
            acc = [None] * tracers
            for k in range(levels):
                m = imp[k, pl.ds(first, rows), :]
                for t in range(tracers):
                    term = m * adj[t, pl.ds(k, 1), :]
                    acc[t] = term if acc[t] is None else acc[t] + term
            mask = wet(first, rows)
            for t in range(tracers):
                value = acc[t] * mask
                carried[t, pl.ds(first, rows), :] = value
                for r in range(0, rows, 8):
                    some = min(8, rows - r)
                    by_row[pl.ds((first + r) * 8 + t, some, stride=8), :] = value[r : r + some]
        if n == 0:
            loads[2].wait()
        for q in range(chunks):
            for s in range(q * CHUNK, min(slots, (q + 1) * CHUNK)):
                row = jnp.minimum(jnp.maximum(rows_ref[s] - me * blocks, 0), blocks - 1)
                hi, lo = split(by_block[row])
                term = jnp.dot(
                    jnp.concatenate([hi, lo], axis=0), tiles[s], preferred_element_type=jnp.float32
                )
                sent[n, q, pl.ds(s % CHUNK, 8, stride=CHUNK), :] = term[:8] + term[8:]
            if n == 0 and q == 0:
                sent[0, 0, pl.ds(body, 8), :] = own_ids
            to_across = copy_of(n, q, sent.at[n, q], ACROSS, across)
            to_partner = copy_of(n, q, sent.at[n, q], PARTNER, partner)
            to_across.start()
            to_partner.start()
            started += [(None, to_across), (None, to_partner)]

        if n == 0:
            loads[3].wait()
        own_sum = placed(own_pick, [sent.at[n]])
        for q in range(chunks):
            for first, rows in level_parts[q * per_chunk : (q + 1) * per_chunk]:
                part = pl.ds(first, rows)
                depth = lax.broadcasted_iota(jnp.int32, (rows, width), 0) + first
                light = jnp.exp(-0.2 * depth.astype(jnp.float32))
                c = [carried[t, part, :] for t in range(tracers)]
                bio = biology(c, [states[section, t, part, :] for t in range(tracers)], light)
                for t in range(tracers):
                    own_part = own_sum[first : first + rows, t * 128 : (t + 1) * 128]
                    adj[t, part, :] = c[t] + own_part + TIME_STEP * bio[t]
            copy_of(n, q, sent.at[n, q], ACROSS, across).wait_recv()
            on = copy_of(n, q, got.at[n, ACROSS, q], RELAYED, relay_to)
            over = copy_of(n, q, got.at[n, ACROSS, q], PASSED, partner)
            pl.when(relays)(on.start)
            pl.when(passes_across)(over.start)
            started += [(relays, on), (passes_across, over)]
        for q in range(chunks):
            copy_of(n, q, sent.at[n, q], PARTNER, partner).wait_recv()
        if n == 0:
            targets = jnp.where(
                lane < slots_pad,
                got[0, PARTNER, 0, pl.ds(body, 8), :],
                got[0, ACROSS, 0, pl.ds(body, 8), :],
            )
            near_pick = pick_of(targets[0:1, : 2 * slots_pad])
        near_sum = placed(near_pick, [got.at[n, PARTNER], got.at[n, ACROSS]])
        for t in range(tracers):
            adj[t] = adj[t] + near_sum[:, t * 128 : (t + 1) * 128]
        for q in range(chunks):
            come = copy_of(n, q, got.at[n, ACROSS, q], RELAYED, relay_to)
            pl.when(relayed)(come.wait_recv)
            over = copy_of(n, q, got.at[n, RELAYED, q], PASSED, partner)
            pl.when(passes_relayed)(over.start)
            started.append((passes_relayed, over))
        for q in range(chunks):
            come = copy_of(n, q, got.at[n, ACROSS, q], PASSED, partner)
            pl.when(gets_passed)(come.wait_recv)
        if n == 0:
            targets = jnp.where(
                lane < slots_pad,
                got[0, RELAYED, 0, pl.ds(body, 8), :],
                got[0, PASSED, 0, pl.ds(body, 8), :],
            )
            far_pick = pick_of(targets[0:1, : 2 * slots_pad])
        far_sum = placed(far_pick, [got.at[n, RELAYED], got.at[n, PASSED]])
        mask = wet(0, levels)
        for t in range(tracers):
            value = mask * (adj[t] + far_sum[:, t * 128 : (t + 1) * 128])
            if n == STEPS - 1:
                out_ref[t] = value
            else:
                adj[t] = value
    for condition, copy in started:
        if condition is None:
            copy.wait_send()
        else:
            pl.when(condition)(copy.wait_send)


def shards(peers, final_adjoint, states, implicit, wet_levels, tile_rows, tile_cols, tiles, tile_count):
    tracers, levels, width = final_adjoint.shape
    blocks = levels * width // 128
    slots = tiles.shape[0]
    chunks = -(-slots // CHUNK)
    rows = (tracers + 1) * CHUNK
    hbm = pl.BlockSpec(memory_space=pl.ANY)
    smem = pl.BlockSpec(memory_space=pltpu.SMEM)
    vmem = pl.BlockSpec(memory_space=pltpu.VMEM)
    f32 = jnp.float32
    return pl.pallas_call(
        functools.partial(kernel, peers, slots, chunks, blocks),
        out_shape=jax.ShapeDtypeStruct((tracers, levels, width), f32),
        in_specs=[hbm, hbm, hbm, vmem, smem, smem, hbm, smem],
        out_specs=vmem,
        scratch_shapes=[
            pltpu.VMEM((tracers, levels, width), f32),
            pltpu.VMEM(states.shape, f32),
            pltpu.VMEM(implicit.shape, f32),
            pltpu.VMEM(tiles.shape, tiles.dtype),
            pltpu.VMEM((tracers, levels, width), f32),
            pltpu.VMEM((blocks, 8, 128), f32),
            pltpu.VMEM((STEPS, chunks, rows, 128), f32),
            pltpu.VMEM((STEPS, 4, chunks, rows, 128), f32),
            pltpu.SemaphoreType.DMA((4,)),
            pltpu.SemaphoreType.DMA((STEPS, 4, chunks)),
            pltpu.SemaphoreType.DMA((STEPS, 4, chunks)),
        ],
        compiler_params=pltpu.CompilerParams(
            collective_id=0, has_side_effects=True, vmem_limit_bytes=60 * 1024 * 1024
        ),
    )(
        final_adjoint, states, implicit, wet_levels.reshape(1, width),
        tile_rows, tile_cols, tiles, tile_count,
    )


def solution(mesh):
    in_specs = (
        P(None, None, "col"),
        P(None, None, None, "col"),
        P(None, None, "col"),
        P("col"),
        P("col"),
        P("col"),
        P("col", None, None),
        P("col"),
    )
    out_specs = P(None, None, "col")
    return jax.shard_map(
        functools.partial(shards, mesh.shape["col"]),
        mesh=mesh, in_specs=in_specs, out_specs=out_specs, check_vma=False,
    )
```

```python
import functools

import jax
import jax.numpy as jnp
from jax import lax
from jax.experimental import pallas as pl
from jax.experimental.pallas import tpu as pltpu
from jax.sharding import PartitionSpec as P

STEPS = 3
REACH = 2
CHUNK = 16
TARGET_ROWS = 8
PARTNER, ACROSS, RELAYED, PASSED = range(4)
TIME_STEP = 0.5


def biology(c, s, light):
    phosphate, _, oxygen, plankton, grazers, detritus, nitrate = s
    inv_p = 1.0 / (0.03 + phosphate)
    inv_n = 1.0 / (0.5 + nitrate)
    inv_o = 1.0 / (1.0 + oxygen)
    square = plankton * plankton
    inv_z = 1.0 / (0.1 + square)
    up = phosphate * inv_p
    un = nitrate * inv_n
    c_growth = -c[0] + 0.1 * c[1] + 1.2 * c[2] + c[3] - 1.6 * c[6]
    c_grazing = 0.3 * c[0] - c[3] + 0.7 * c[4]
    c_mortality = 0.1 * c[1] - c[3] + 0.9 * c[5]
    c_remineral = c[0] - 1.2 * c[2] - c[5] + 1.6 * c[6]
    c_decay = c[0] - c[1] - 1.2 * c[2] + 1.6 * c[6]
    c_loss = c[5] - c[4]
    g = c_growth * (1.2 * light)
    gz = g * plankton
    q = 0.05 * c_remineral
    return (
        gz * un * (0.03 * inv_p * inv_p),
        0.17 * c_decay,
        q * detritus * (inv_o * inv_o),
        g * up * un
        + c_grazing * grazers * plankton * (0.38 * inv_z * inv_z)
        + 0.06 * c_mortality * plankton,
        1.9 * c_grazing * square * inv_z + 0.1 * c_loss * grazers,
        q * oxygen * inv_o,
        gz * up * (0.5 * inv_n * inv_n),
    )


def split(x):
    hi = x.astype(jnp.bfloat16)
    lo = (x - hi.astype(jnp.float32)).astype(jnp.bfloat16)
    return hi, lo


def tracer_groups(tracers):
    half = (tracers + 1) // 2
    return [(0, half), (half, tracers)]


def kernel(
    peers, slots, chunks, blocks,
    adj_hbm, states_hbm, imp_hbm, wet_ref, rows_ref, cols_ref, tiles_hbm, count_ref,
    early_ref, late_ref,
    adj, states, imp, tiles, carried, by_block, sent, got,
    load_sem, send_sem, recv_sem, pass_sem,
):
    tracers, levels, width = adj.shape
    groups = tracer_groups(tracers)
    half = groups[0][1]
    slots_pad = chunks * CHUNK
    body = half * CHUNK
    by_row = by_block.reshape(2, blocks * 8, 128)
    me = lax.axis_index("col")
    chip = me // 2
    core = me % 2
    odd = chip % 2
    partner = me + 1 - 2 * core
    across = me + 2 - 4 * odd
    relay_to = me + 4 - 8 * odd
    relay_from = me - 4 + 8 * odd
    beside = me - 1 + 2 * odd
    relays = (relay_to >= 0) & (relay_to < peers)
    relayed = (relay_from >= 0) & (relay_from < peers)
    passes = core == odd
    direct = passes & relayed
    gets_fourth = jnp.logical_not(passes) | relayed
    misses_fourth = passes & jnp.logical_not(relayed)

    loads = [
        pltpu.make_async_copy(src, dst, load_sem.at[i])
        for i, (src, dst) in enumerate(
            ((adj_hbm, adj), (imp_hbm, imp), (tiles_hbm, tiles), (states_hbm, states))
        )
    ]
    for load in loads:
        load.start()

    barrier = pltpu.get_barrier_semaphore()

    def greet(device):
        pl.semaphore_signal(
            barrier, inc=1, device_id=(device,), device_id_type=pl.DeviceIdType.MESH
        )

    greet(partner)
    greet(across)
    pl.when(relays)(lambda: greet(relay_to))
    pl.when(relayed)(lambda: greet(relay_from))
    pl.when(direct)(lambda: greet(beside))

    lane = lax.broadcasted_iota(jnp.int32, (TARGET_ROWS, 128), 1)
    lane_slot = lane % slots_pad
    own_ids = jnp.full((TARGET_ROWS, 128), -1, jnp.int32)
    for s in range(slots):
        own_ids = jnp.where(lane_slot == s, cols_ref[s], own_ids)
    own_ids = jnp.where(lane_slot < count_ref[0], own_ids, -1).astype(jnp.float32)
    for n in range(STEPS):
        for g in range(2):
            for s in range(slots, slots_pad):
                sent[n, g, s // CHUNK, pl.ds(s % CHUNK, half, stride=CHUNK), :] = jnp.zeros(
                    (half, 128), jnp.float32
                )
    for g in range(2):
        count = groups[g][1] - groups[g][0]
        for r in list(range(count, half)) + list(range(half + count, 8)):
            for first in range(0, blocks, 8):
                some = min(8, blocks - first)
                by_row[g, pl.ds(first * 8 + r, some, stride=8), :] = jnp.zeros(
                    (some, 128), jnp.float32
                )

    def blank(place):
        for n in range(STEPS):
            for g in range(2):
                for q in range(chunks):
                    got[n, place, g, q] = jnp.zeros(got.shape[4:], jnp.float32)
        got[0, place, 0, 0, pl.ds(body, TARGET_ROWS), :] = jnp.full(
            (TARGET_ROWS, 128), -1.0, jnp.float32
        )

    pl.when(jnp.logical_not(relayed))(lambda: blank(RELAYED))
    pl.when(misses_fourth)(lambda: blank(PASSED))

    pl.semaphore_wait(
        barrier,
        2 + relays.astype(jnp.int32) + relayed.astype(jnp.int32) + direct.astype(jnp.int32),
    )

    def copy_of(n, g, q, source, place, device, sem=None):
        size = (groups[g][1] - groups[g][0]) * CHUNK
        if n == 0 and g == 0 and q == 0:
            size = body + TARGET_ROWS
        return pltpu.make_async_remote_copy(
            src_ref=source.at[g, q, pl.ds(0, size)],
            dst_ref=got.at[n, place, g, q, pl.ds(0, size)],
            send_sem=send_sem.at[n, place, g, q] if sem is None else sem,
            recv_sem=recv_sem.at[n, place, g, q],
            device_id=(device,), device_id_type=pl.DeviceIdType.MESH,
        )

    def wet(first, rows):
        level = lax.broadcasted_iota(jnp.int32, (rows, width), 0) + first
        return (level < wet_ref[...]).astype(jnp.float32)

    def pick_of(targets):
        block = lax.broadcasted_iota(jnp.int32, (blocks, targets.shape[1]), 0) + me * blocks
        pick = (block.astype(jnp.float32) == targets).astype(jnp.bfloat16)
        return jnp.concatenate([pick, pick], axis=1)

    def placed(pick, g, sources):
        columns = []
        for t in range(groups[g][1] - groups[g][0]):
            pieces = [
                ref[g, q, pl.ds(t * CHUNK, CHUNK), :] for ref in sources for q in range(chunks)
            ]
            columns.append(jnp.concatenate(split(jnp.concatenate(pieces, axis=0)), axis=0))
        return jnp.dot(pick, jnp.concatenate(columns, axis=1), preferred_element_type=jnp.float32)

    started = []
    picks = {}

    def compute(n, g):
        begin, end = groups[g]
        acc = [None] * (end - begin)
        for k in range(levels):
            m = imp[k]
            for t in range(begin, end):
                term = m * adj[t, pl.ds(k, 1), :]
                acc[t - begin] = term if k == 0 else acc[t - begin] + term
        mask = wet(0, levels)
        for t in range(begin, end):
            value = acc[t - begin] * mask
            carried[t] = value
            hi, lo = split(value)
            for piece, row in ((hi, t - begin), (lo, t - begin + half)):
                piece = piece.astype(jnp.float32)
                for r in range(0, levels, 8):
                    some = min(8, levels - r)
                    by_row[g, pl.ds(r * 8 + row, some, stride=8), :] = piece[r : r + some]
        if n == 0 and g == 0:
            loads[2].wait()
        for q in range(chunks):
            for s in range(q * CHUNK, min(slots, (q + 1) * CHUNK)):
                row = jnp.minimum(jnp.maximum(rows_ref[s] - me * blocks, 0), blocks - 1)
                both = jnp.dot(
                    by_block[g, row].astype(jnp.bfloat16), tiles[s],
                    preferred_element_type=jnp.float32,
                )
                sent[n, g, q, pl.ds(s % CHUNK, half, stride=CHUNK), :] = (
                    both[:half] + both[half : 2 * half]
                )
            if n == 0 and g == 0 and q == 0:
                sent[0, 0, 0, pl.ds(body, TARGET_ROWS), :] = own_ids
            copy = copy_of(n, g, q, sent.at[n], ACROSS, across)
            copy.start()
            started.append((None, copy))
        for q in range(chunks):
            near = copy_of(n, g, q, sent.at[n], PARTNER, partner)
            near.start()
            far = copy_of(n, g, q, sent.at[n], PASSED, beside)
            pl.when(direct)(far.start)
            started.extend([(None, near), (direct, far)])

    def grow(n):
        section = STEPS - 1 - n
        if n == 0:
            loads[3].wait()
        for first in range(0, levels, 8):
            rows = min(8, levels - first)
            part = pl.ds(first, rows)
            depth = lax.broadcasted_iota(jnp.int32, (rows, width), 0) + first
            light = jnp.exp(-0.2 * depth.astype(jnp.float32))
            c = [carried[t, part, :] for t in range(tracers)]
            bio = biology(c, [states[section, t, part, :] for t in range(tracers)], light)
            for t in range(tracers):
                adj[t, part, :] = c[t] + TIME_STEP * bio[t]

    def forward(n, g):
        for q in range(chunks):
            copy_of(n, g, q, sent.at[n], ACROSS, across).wait_recv()
            on = copy_of(n, g, q, got.at[n, ACROSS], RELAYED, relay_to)
            over = copy_of(n, g, q, got.at[n, ACROSS], PASSED, partner, pass_sem.at[n, g, q])
            pl.when(relays)(on.start)
            pl.when(passes)(over.start)
            started.extend([(relays, on), (passes, over)])

    def two(n, first, second):
        return jnp.where(
            lane < slots_pad,
            first[0, 0, pl.ds(body, TARGET_ROWS), :],
            second[0, 0, pl.ds(body, TARGET_ROWS), :],
        )

    def near(n, g):
        for q in range(chunks):
            copy_of(n, g, q, sent.at[n], PARTNER, partner).wait_recv()
        if "near" not in picks:
            ids = two(n, sent.at[0], got.at[0, PARTNER])
            ids = jnp.where(
                lane < 2 * slots_pad, ids, got[0, ACROSS, 0, 0, pl.ds(body, TARGET_ROWS), :]
            )
            picks["near"] = pick_of(ids[0:1, : 3 * slots_pad])
        total = placed(
            picks["near"], g, [sent.at[n], got.at[n, PARTNER], got.at[n, ACROSS]]
        )
        for i, t in enumerate(range(*groups[g])):
            adj[t] = adj[t] + total[:, i * 128 : (i + 1) * 128]

    def finish(n, g):
        for q in range(chunks):
            come = copy_of(n, g, q, got.at[n, ACROSS], RELAYED, relay_to)
            pl.when(relayed)(come.wait_recv)
            fourth = copy_of(n, g, q, sent.at[n], PASSED, beside)
            pl.when(gets_fourth)(fourth.wait_recv)
        if "far" not in picks:
            ids = two(n, got.at[0, RELAYED], got.at[0, PASSED])
            picks["far"] = pick_of(ids[0:1, : 2 * slots_pad])
        total = placed(picks["far"], g, [got.at[n, RELAYED], got.at[n, PASSED]])
        mask = wet(0, levels)
        for i, t in enumerate(range(*groups[g])):
            late = total[:, i * 128 : (i + 1) * 128]
            if n == STEPS - 1:
                early_ref[t] = mask * adj[t]
                late_ref[t] = mask * late
            else:
                adj[t] = mask * (adj[t] + late)

    loads[0].wait()
    loads[1].wait()
    compute(0, 0)
    compute(0, 1)
    grow(0)
    for n in range(STEPS):
        forward(n, 0)
        near(n, 0)
        forward(n, 1)
        near(n, 1)
        finish(n, 0)
        if n < STEPS - 1:
            compute(n + 1, 0)
        finish(n, 1)
        if n < STEPS - 1:
            compute(n + 1, 1)
            grow(n + 1)
    for condition, copy in started:
        if condition is None:
            copy.wait_send()
        else:
            pl.when(condition)(copy.wait_send)


def shards(peers, final_adjoint, states, implicit, wet_levels, tile_rows, tile_cols, tiles, tile_count):
    tracers, levels, width = final_adjoint.shape
    blocks = levels * width // 128
    slots = tiles.shape[0]
    chunks = -(-slots // CHUNK)
    rows = tracer_groups(tracers)[0][1] * CHUNK + TARGET_ROWS
    hbm = pl.BlockSpec(memory_space=pl.ANY)
    smem = pl.BlockSpec(memory_space=pltpu.SMEM)
    vmem = pl.BlockSpec(memory_space=pltpu.VMEM)
    f32 = jnp.float32
    early, late = pl.pallas_call(
        functools.partial(kernel, peers, slots, chunks, blocks),
        out_shape=[jax.ShapeDtypeStruct((tracers, levels, width), f32)] * 2,
        in_specs=[hbm, hbm, hbm, vmem, smem, smem, hbm, smem],
        out_specs=[vmem, vmem],
        scratch_shapes=[
            pltpu.VMEM((tracers, levels, width), f32),
            pltpu.VMEM(states.shape, f32),
            pltpu.VMEM(implicit.shape, f32),
            pltpu.VMEM(tiles.shape, tiles.dtype),
            pltpu.VMEM((tracers, levels, width), f32),
            pltpu.VMEM((2, blocks, 8, 128), f32),
            pltpu.VMEM((STEPS, 2, chunks, rows, 128), f32),
            pltpu.VMEM((STEPS, 4, 2, chunks, rows, 128), f32),
            pltpu.SemaphoreType.DMA((4,)),
            pltpu.SemaphoreType.DMA((STEPS, 4, 2, chunks)),
            pltpu.SemaphoreType.DMA((STEPS, 4, 2, chunks)),
            pltpu.SemaphoreType.DMA((STEPS, 2, chunks)),
        ],
        compiler_params=pltpu.CompilerParams(
            collective_id=0, has_side_effects=True, vmem_limit_bytes=60 * 1024 * 1024
        ),
    )(
        final_adjoint, states, implicit, wet_levels.reshape(1, width),
        tile_rows, tile_cols, tiles, tile_count,
    )
    return early + late


def solution(mesh):
    in_specs = (
        P(None, None, "col"),
        P(None, None, None, "col"),
        P(None, None, "col"),
        P("col"),
        P("col"),
        P("col"),
        P("col", None, None),
        P("col"),
    )
    out_specs = P(None, None, "col")
    return jax.shard_map(
        functools.partial(shards, mesh.shape["col"]),
        mesh=mesh, in_specs=in_specs, out_specs=out_specs, check_vma=False,
    )
```

```python
import functools

import jax
import jax.numpy as jnp
from jax import lax
from jax.experimental import pallas as pl
from jax.experimental.pallas import tpu as pltpu
from jax.sharding import PartitionSpec as P

STEPS = 3
REACH = 2
CHUNK = 16
TARGET_ROWS = 8
PARTNER, ACROSS, RELAYED, PASSED = range(4)
TIME_STEP = 0.5


def biology(c, s, light):
    phosphate, _, oxygen, plankton, grazers, detritus, nitrate = s
    inv_p = 1.0 / (0.03 + phosphate)
    inv_n = 1.0 / (0.5 + nitrate)
    inv_o = 1.0 / (1.0 + oxygen)
    square = plankton * plankton
    inv_z = 1.0 / (0.1 + square)
    up = phosphate * inv_p
    un = nitrate * inv_n
    c_growth = -c[0] + 0.1 * c[1] + 1.2 * c[2] + c[3] - 1.6 * c[6]
    c_grazing = 0.3 * c[0] - c[3] + 0.7 * c[4]
    c_mortality = 0.1 * c[1] - c[3] + 0.9 * c[5]
    c_remineral = c[0] - 1.2 * c[2] - c[5] + 1.6 * c[6]
    c_decay = c[0] - c[1] - 1.2 * c[2] + 1.6 * c[6]
    c_loss = c[5] - c[4]
    g = c_growth * (1.2 * light)
    gz = g * plankton
    q = 0.05 * c_remineral
    return (
        gz * un * (0.03 * inv_p * inv_p),
        0.17 * c_decay,
        q * detritus * (inv_o * inv_o),
        g * up * un
        + c_grazing * grazers * plankton * (0.38 * inv_z * inv_z)
        + 0.06 * c_mortality * plankton,
        1.9 * c_grazing * square * inv_z + 0.1 * c_loss * grazers,
        q * oxygen * inv_o,
        gz * up * (0.5 * inv_n * inv_n),
    )


def split(x):
    hi = x.astype(jnp.bfloat16)
    lo = (x - hi.astype(jnp.float32)).astype(jnp.bfloat16)
    return hi, lo


def tracer_groups(tracers):
    half = (tracers + 1) // 2
    return [(0, half), (half, tracers)]


def kernel(
    peers, slots, chunks, blocks,
    adj_hbm, states_hbm, imp_hbm, wet_ref, rows_ref, cols_ref, tiles_hbm, count_ref,
    early_ref, late_ref,
    adj, states, imp, tiles, carried, by_block, sent, got,
    load_sem, send_sem, recv_sem, pass_sem,
):
    tracers, levels, width = adj.shape
    groups = tracer_groups(tracers)
    half = groups[0][1]
    slots_pad = chunks * CHUNK
    body = half * CHUNK
    by_row = by_block.reshape(2, blocks * 8, 128)
    me = lax.axis_index("col")
    chip = me // 2
    core = me % 2
    odd = chip % 2
    partner = me + 1 - 2 * core
    across = me + 2 - 4 * odd
    relay_to = me + 4 - 8 * odd
    relay_from = me - 4 + 8 * odd
    beside = me - 1 + 2 * odd
    relays = (relay_to >= 0) & (relay_to < peers)
    relayed = (relay_from >= 0) & (relay_from < peers)
    passes = core == odd
    direct = passes & relayed
    gets_fourth = jnp.logical_not(passes) | relayed
    misses_fourth = passes & jnp.logical_not(relayed)

    loads = [
        pltpu.make_async_copy(src, dst, load_sem.at[i])
        for i, (src, dst) in enumerate(
            ((adj_hbm, adj), (imp_hbm, imp), (tiles_hbm, tiles), (states_hbm, states))
        )
    ]
    for load in loads:
        load.start()

    barrier = pltpu.get_barrier_semaphore()

    def greet(device):
        pl.semaphore_signal(
            barrier, inc=1, device_id=(device,), device_id_type=pl.DeviceIdType.MESH
        )

    greet(partner)
    greet(across)
    pl.when(relays)(lambda: greet(relay_to))
    pl.when(relayed)(lambda: greet(relay_from))
    pl.when(direct)(lambda: greet(beside))

    lane = lax.broadcasted_iota(jnp.int32, (TARGET_ROWS, 128), 1)
    lane_slot = lane % slots_pad
    own_ids = jnp.full((TARGET_ROWS, 128), -1, jnp.int32)
    for s in range(slots):
        own_ids = jnp.where(lane_slot == s, cols_ref[s], own_ids)
    own_ids = jnp.where(lane_slot < count_ref[0], own_ids, -1).astype(jnp.float32)
    for n in range(STEPS):
        for g in range(2):
            for s in range(slots, slots_pad):
                sent[n, g, s // CHUNK, pl.ds(s % CHUNK, half, stride=CHUNK), :] = jnp.zeros(
                    (half, 128), jnp.float32
                )
    for g in range(2):
        count = groups[g][1] - groups[g][0]
        for r in list(range(count, half)) + list(range(half + count, 8)):
            for first in range(0, blocks, 8):
                some = min(8, blocks - first)
                by_row[g, pl.ds(first * 8 + r, some, stride=8), :] = jnp.zeros(
                    (some, 128), jnp.float32
                )

    def blank(place):
        for n in range(STEPS):
            for g in range(2):
                for q in range(chunks):
                    got[n, place, g, q] = jnp.zeros(got.shape[4:], jnp.float32)
        got[0, place, 0, 0, pl.ds(body, TARGET_ROWS), :] = jnp.full(
            (TARGET_ROWS, 128), -1.0, jnp.float32
        )

    pl.when(jnp.logical_not(relayed))(lambda: blank(RELAYED))
    pl.when(misses_fourth)(lambda: blank(PASSED))

    pl.semaphore_wait(
        barrier,
        2 + relays.astype(jnp.int32) + relayed.astype(jnp.int32) + direct.astype(jnp.int32),
    )

    def copy_of(n, g, q, source, place, device, sem=None):
        size = (groups[g][1] - groups[g][0]) * CHUNK
        if n == 0 and g == 0 and q == 0:
            size = body + TARGET_ROWS
        return pltpu.make_async_remote_copy(
            src_ref=source.at[g, q, pl.ds(0, size)],
            dst_ref=got.at[n, place, g, q, pl.ds(0, size)],
            send_sem=send_sem.at[n, place, g, q] if sem is None else sem,
            recv_sem=recv_sem.at[n, place, g, q],
            device_id=(device,), device_id_type=pl.DeviceIdType.MESH,
        )

    def wet(first, rows):
        level = lax.broadcasted_iota(jnp.int32, (rows, width), 0) + first
        return (level < wet_ref[...]).astype(jnp.float32)

    def pick_of(targets):
        block = lax.broadcasted_iota(jnp.int32, (blocks, targets.shape[1]), 0) + me * blocks
        pick = (block.astype(jnp.float32) == targets).astype(jnp.bfloat16)
        return jnp.concatenate([pick, pick], axis=1)

    def placed(pick, g, sources):
        columns = []
        for t in range(groups[g][1] - groups[g][0]):
            pieces = [
                ref[g, q, pl.ds(t * CHUNK, CHUNK), :] for ref in sources for q in range(chunks)
            ]
            columns.append(jnp.concatenate(split(jnp.concatenate(pieces, axis=0)), axis=0))
        return jnp.dot(pick, jnp.concatenate(columns, axis=1), preferred_element_type=jnp.float32)

    started = []
    picks = {}

    def compute(n, g):
        begin, end = groups[g]
        acc = [None] * (end - begin)
        for k in range(levels):
            m = imp[k]
            for t in range(begin, end):
                term = m * adj[t, pl.ds(k, 1), :]
                acc[t - begin] = term if k == 0 else acc[t - begin] + term
        mask = wet(0, levels)
        for t in range(begin, end):
            value = acc[t - begin] * mask
            carried[t] = value
            hi, lo = split(value)
            for piece, row in ((hi, t - begin), (lo, t - begin + half)):
                piece = piece.astype(jnp.float32)
                for r in range(0, levels, 8):
                    some = min(8, levels - r)
                    by_row[g, pl.ds(r * 8 + row, some, stride=8), :] = piece[r : r + some]
        if n == 0 and g == 0:
            loads[2].wait()
        for q in range(chunks):
            last = min(slots, (q + 1) * CHUNK)
            for s in range(q * CHUNK, last, 4):
                some = list(range(s, min(s + 4, last)))
                zero = jnp.zeros((8, 128), jnp.bfloat16)
                lines, sides = [], []
                for i, slot in enumerate(some):
                    row = jnp.minimum(jnp.maximum(rows_ref[slot] - me * blocks, 0), blocks - 1)
                    x = by_block[g, row].astype(jnp.bfloat16)
                    lines.append(jnp.concatenate([zero, x] if i % 2 else [x, zero], axis=1))
                for i in range(0, len(some), 2):
                    pair = [tiles[slot] for slot in some[i : i + 2]]
                    if len(pair) == 1:
                        pair.append(jnp.zeros_like(pair[0]))
                    sides.append(jnp.concatenate(pair, axis=0))
                product = jnp.dot(
                    jnp.concatenate(lines, axis=0), jnp.concatenate(sides, axis=1),
                    preferred_element_type=jnp.float32,
                )
                for i, slot in enumerate(some):
                    both = product[8 * i : 8 * i + 8, i // 2 * 128 : i // 2 * 128 + 128]
                    sent[n, g, q, pl.ds(slot % CHUNK, half, stride=CHUNK), :] = (
                        both[:half] + both[half : 2 * half]
                    )
            if n == 0 and g == 0 and q == 0:
                sent[0, 0, 0, pl.ds(body, TARGET_ROWS), :] = own_ids
            copy = copy_of(n, g, q, sent.at[n], ACROSS, across)
            copy.start()
            started.append((None, copy))
        for q in range(chunks):
            near = copy_of(n, g, q, sent.at[n], PARTNER, partner)
            near.start()
            far = copy_of(n, g, q, sent.at[n], PASSED, beside)
            pl.when(direct)(far.start)
            started.extend([(None, near), (direct, far)])

    def grow(n):
        section = STEPS - 1 - n
        if n == 0:
            loads[3].wait()
        for first in range(0, levels, 8):
            rows = min(8, levels - first)
            part = pl.ds(first, rows)
            depth = lax.broadcasted_iota(jnp.int32, (rows, width), 0) + first
            light = jnp.exp(-0.2 * depth.astype(jnp.float32))
            c = [carried[t, part, :] for t in range(tracers)]
            bio = biology(c, [states[section, t, part, :] for t in range(tracers)], light)
            for t in range(tracers):
                adj[t, part, :] = c[t] + TIME_STEP * bio[t]

    def forward(n, g):
        for q in range(chunks):
            copy_of(n, g, q, sent.at[n], ACROSS, across).wait_recv()
            on = copy_of(n, g, q, got.at[n, ACROSS], RELAYED, relay_to)
            over = copy_of(n, g, q, got.at[n, ACROSS], PASSED, partner, pass_sem.at[n, g, q])
            pl.when(relays)(on.start)
            pl.when(passes)(over.start)
            started.extend([(relays, on), (passes, over)])

    def two(n, first, second):
        return jnp.where(
            lane < slots_pad,
            first[0, 0, pl.ds(body, TARGET_ROWS), :],
            second[0, 0, pl.ds(body, TARGET_ROWS), :],
        )

    def near(n, g):
        for q in range(chunks):
            copy_of(n, g, q, sent.at[n], PARTNER, partner).wait_recv()
        if "near" not in picks:
            ids = two(n, sent.at[0], got.at[0, PARTNER])
            ids = jnp.where(
                lane < 2 * slots_pad, ids, got[0, ACROSS, 0, 0, pl.ds(body, TARGET_ROWS), :]
            )
            picks["near"] = pick_of(ids[0:1, : 3 * slots_pad])
        total = placed(
            picks["near"], g, [sent.at[n], got.at[n, PARTNER], got.at[n, ACROSS]]
        )
        for i, t in enumerate(range(*groups[g])):
            adj[t] = adj[t] + total[:, i * 128 : (i + 1) * 128]

    def finish(n, g):
        for q in range(chunks):
            come = copy_of(n, g, q, got.at[n, ACROSS], RELAYED, relay_to)
            pl.when(relayed)(come.wait_recv)
            fourth = copy_of(n, g, q, sent.at[n], PASSED, beside)
            pl.when(gets_fourth)(fourth.wait_recv)
        if "far" not in picks:
            ids = two(n, got.at[0, RELAYED], got.at[0, PASSED])
            picks["far"] = pick_of(ids[0:1, : 2 * slots_pad])
        total = placed(picks["far"], g, [got.at[n, RELAYED], got.at[n, PASSED]])
        mask = wet(0, levels)
        for i, t in enumerate(range(*groups[g])):
            late = total[:, i * 128 : (i + 1) * 128]
            if n == STEPS - 1:
                early_ref[t] = mask * adj[t]
                late_ref[t] = mask * late
            else:
                adj[t] = mask * (adj[t] + late)

    loads[0].wait()
    loads[1].wait()
    compute(0, 0)
    compute(0, 1)
    grow(0)
    for n in range(STEPS):
        forward(n, 0)
        near(n, 0)
        forward(n, 1)
        near(n, 1)
        finish(n, 0)
        if n < STEPS - 1:
            compute(n + 1, 0)
        finish(n, 1)
        if n < STEPS - 1:
            compute(n + 1, 1)
            grow(n + 1)
    for condition, copy in started:
        if condition is None:
            copy.wait_send()
        else:
            pl.when(condition)(copy.wait_send)


def shards(peers, final_adjoint, states, implicit, wet_levels, tile_rows, tile_cols, tiles, tile_count):
    tracers, levels, width = final_adjoint.shape
    blocks = levels * width // 128
    slots = tiles.shape[0]
    chunks = -(-slots // CHUNK)
    rows = tracer_groups(tracers)[0][1] * CHUNK + TARGET_ROWS
    hbm = pl.BlockSpec(memory_space=pl.ANY)
    smem = pl.BlockSpec(memory_space=pltpu.SMEM)
    vmem = pl.BlockSpec(memory_space=pltpu.VMEM)
    f32 = jnp.float32
    early, late = pl.pallas_call(
        functools.partial(kernel, peers, slots, chunks, blocks),
        out_shape=[jax.ShapeDtypeStruct((tracers, levels, width), f32)] * 2,
        in_specs=[hbm, hbm, hbm, vmem, smem, smem, hbm, smem],
        out_specs=[vmem, vmem],
        scratch_shapes=[
            pltpu.VMEM((tracers, levels, width), f32),
            pltpu.VMEM(states.shape, f32),
            pltpu.VMEM(implicit.shape, f32),
            pltpu.VMEM(tiles.shape, tiles.dtype),
            pltpu.VMEM((tracers, levels, width), f32),
            pltpu.VMEM((2, blocks, 8, 128), f32),
            pltpu.VMEM((STEPS, 2, chunks, rows, 128), f32),
            pltpu.VMEM((STEPS, 4, 2, chunks, rows, 128), f32),
            pltpu.SemaphoreType.DMA((4,)),
            pltpu.SemaphoreType.DMA((STEPS, 4, 2, chunks)),
            pltpu.SemaphoreType.DMA((STEPS, 4, 2, chunks)),
            pltpu.SemaphoreType.DMA((STEPS, 2, chunks)),
        ],
        compiler_params=pltpu.CompilerParams(
            collective_id=0, has_side_effects=True, vmem_limit_bytes=60 * 1024 * 1024
        ),
    )(
        final_adjoint, states, implicit, wet_levels.reshape(1, width),
        tile_rows, tile_cols, tiles, tile_count,
    )
    return early + late


def solution(mesh):
    in_specs = (
        P(None, None, "col"),
        P(None, None, None, "col"),
        P(None, None, "col"),
        P("col"),
        P("col"),
        P("col"),
        P("col", None, None),
        P("col"),
    )
    out_specs = P(None, None, "col")
    return jax.shard_map(
        functools.partial(shards, mesh.shape["col"]),
        mesh=mesh, in_specs=in_specs, out_specs=out_specs, check_vma=False,
    )
```

```python
import functools

import jax
import jax.numpy as jnp
from jax import lax
from jax.experimental import pallas as pl
from jax.experimental.pallas import tpu as pltpu
from jax.sharding import PartitionSpec as P

STEPS = 3
REACH = 2
CHUNK = 16
TARGET_ROWS = 8
PARTNER, ACROSS, RELAYED, PASSED = range(4)
TIME_STEP = 0.5


def biology(c, s, light):
    phosphate, _, oxygen, plankton, grazers, detritus, nitrate = s
    inv_p = 1.0 / (0.03 + phosphate)
    inv_n = 1.0 / (0.5 + nitrate)
    inv_o = 1.0 / (1.0 + oxygen)
    square = plankton * plankton
    inv_z = 1.0 / (0.1 + square)
    up = phosphate * inv_p
    un = nitrate * inv_n
    c_growth = -c[0] + 0.1 * c[1] + 1.2 * c[2] + c[3] - 1.6 * c[6]
    c_grazing = 0.3 * c[0] - c[3] + 0.7 * c[4]
    c_mortality = 0.1 * c[1] - c[3] + 0.9 * c[5]
    c_remineral = c[0] - 1.2 * c[2] - c[5] + 1.6 * c[6]
    c_decay = c[0] - c[1] - 1.2 * c[2] + 1.6 * c[6]
    c_loss = c[5] - c[4]
    g = c_growth * (1.2 * light)
    gz = g * plankton
    q = 0.05 * c_remineral
    return (
        gz * un * (0.03 * inv_p * inv_p),
        0.17 * c_decay,
        q * detritus * (inv_o * inv_o),
        g * up * un
        + c_grazing * grazers * plankton * (0.38 * inv_z * inv_z)
        + 0.06 * c_mortality * plankton,
        1.9 * c_grazing * square * inv_z + 0.1 * c_loss * grazers,
        q * oxygen * inv_o,
        gz * up * (0.5 * inv_n * inv_n),
    )


def split(x):
    hi = x.astype(jnp.bfloat16)
    lo = (x - hi.astype(jnp.float32)).astype(jnp.bfloat16)
    return hi, lo


def tracer_groups(tracers):
    half = (tracers + 1) // 2
    return [(0, half), (half, tracers)]


def kernel(
    peers, slots, chunks, blocks,
    adj_hbm, states_hbm, imp_hbm, wet_ref, rows_ref, cols_ref, tiles_hbm, count_ref,
    out_ref,
    adj, states, imp, tiles, carried, by_block, sent, got,
    load_sem, send_sem, recv_sem, pass_sem,
):
    tracers, levels, width = adj.shape
    groups = tracer_groups(tracers)
    half = groups[0][1]
    slots_pad = chunks * CHUNK
    body = half * CHUNK
    by_row = by_block.reshape(2, blocks * 8, 128)
    me = lax.axis_index("col")
    chip = me // 2
    core = me % 2
    odd = chip % 2
    partner = me + 1 - 2 * core
    across = me + 2 - 4 * odd
    relay_to = me + 4 - 8 * odd
    relay_from = me - 4 + 8 * odd
    relays = (relay_to >= 0) & (relay_to < peers)
    relayed = (relay_from >= 0) & (relay_from < peers)
    passes = core == odd
    passes_relayed = jnp.logical_not(passes) & relayed
    gets_fourth = jnp.logical_not(passes) | relayed
    misses_fourth = passes & jnp.logical_not(relayed)

    loads = [
        pltpu.make_async_copy(src, dst, load_sem.at[i])
        for i, (src, dst) in enumerate(
            ((adj_hbm, adj), (imp_hbm, imp), (tiles_hbm, tiles), (states_hbm, states))
        )
    ]
    for load in loads:
        load.start()

    barrier = pltpu.get_barrier_semaphore()

    def greet(device):
        pl.semaphore_signal(
            barrier, inc=1, device_id=(device,), device_id_type=pl.DeviceIdType.MESH
        )

    greet(partner)
    greet(across)
    pl.when(relays)(lambda: greet(relay_to))
    pl.when(relayed)(lambda: greet(relay_from))

    lane = lax.broadcasted_iota(jnp.int32, (TARGET_ROWS, 128), 1)
    lane_slot = lane % slots_pad
    own_ids = jnp.full((TARGET_ROWS, 128), -1, jnp.int32)
    for s in range(slots):
        own_ids = jnp.where(lane_slot == s, cols_ref[s], own_ids)
    own_ids = jnp.where(lane_slot < count_ref[0], own_ids, -1).astype(jnp.float32)
    for n in range(STEPS):
        for g in range(2):
            for s in range(slots, slots_pad):
                sent[n, g, s // CHUNK, pl.ds(s % CHUNK, half, stride=CHUNK), :] = jnp.zeros(
                    (half, 128), jnp.float32
                )
    for g in range(2):
        count = groups[g][1] - groups[g][0]
        for r in list(range(count, half)) + list(range(half + count, 8)):
            for first in range(0, blocks, 8):
                some = min(8, blocks - first)
                by_row[g, pl.ds(first * 8 + r, some, stride=8), :] = jnp.zeros(
                    (some, 128), jnp.float32
                )

    def blank(place):
        for n in range(STEPS):
            for g in range(2):
                for q in range(chunks):
                    got[n, place, g, q] = jnp.zeros(got.shape[4:], jnp.float32)
        got[0, place, 0, 0, pl.ds(body, TARGET_ROWS), :] = jnp.full(
            (TARGET_ROWS, 128), -1.0, jnp.float32
        )

    pl.when(jnp.logical_not(relayed))(lambda: blank(RELAYED))
    pl.when(misses_fourth)(lambda: blank(PASSED))

    pl.semaphore_wait(
        barrier,
        2 + relays.astype(jnp.int32) + relayed.astype(jnp.int32),
    )

    def copy_of(n, g, q, source, place, device, sem=None):
        size = (groups[g][1] - groups[g][0]) * CHUNK
        if n == 0 and g == 0 and q == 0:
            size = body + TARGET_ROWS
        return pltpu.make_async_remote_copy(
            src_ref=source.at[g, q, pl.ds(0, size)],
            dst_ref=got.at[n, place, g, q, pl.ds(0, size)],
            send_sem=send_sem.at[n, place, g, q] if sem is None else sem,
            recv_sem=recv_sem.at[n, place, g, q],
            device_id=(device,), device_id_type=pl.DeviceIdType.MESH,
        )

    def wet(first, rows):
        level = lax.broadcasted_iota(jnp.int32, (rows, width), 0) + first
        return (level < wet_ref[...]).astype(jnp.float32)

    def pick_of(targets):
        block = lax.broadcasted_iota(jnp.int32, (blocks, targets.shape[1]), 0) + me * blocks
        pick = (block.astype(jnp.float32) == targets).astype(jnp.bfloat16)
        return jnp.concatenate([pick, pick], axis=1)

    def placed(pick, g, sources):
        columns = []
        for t in range(groups[g][1] - groups[g][0]):
            pieces = [
                ref[g, q, pl.ds(t * CHUNK, CHUNK), :] for ref in sources for q in range(chunks)
            ]
            columns.append(jnp.concatenate(split(jnp.concatenate(pieces, axis=0)), axis=0))
        return jnp.dot(pick, jnp.concatenate(columns, axis=1), preferred_element_type=jnp.float32)

    started = []
    picks = {}

    def compute(n, g):
        begin, end = groups[g]
        acc = [None] * (end - begin)
        for k in range(levels):
            m = imp[k]
            for t in range(begin, end):
                term = m * adj[t, pl.ds(k, 1), :]
                acc[t - begin] = term if k == 0 else acc[t - begin] + term
        mask = wet(0, levels)
        for t in range(begin, end):
            value = acc[t - begin] * mask
            carried[t] = value
            hi, lo = split(value)
            for piece, row in ((hi, t - begin), (lo, t - begin + half)):
                piece = piece.astype(jnp.float32)
                for r in range(0, levels, 8):
                    some = min(8, levels - r)
                    by_row[g, pl.ds(r * 8 + row, some, stride=8), :] = piece[r : r + some]
        if n == 0 and g == 0:
            loads[2].wait()
        for q in range(chunks):
            last = min(slots, (q + 1) * CHUNK)
            for s in range(q * CHUNK, last, 4):
                some = list(range(s, min(s + 4, last)))
                zero = jnp.zeros((8, 128), jnp.bfloat16)
                lines, sides = [], []
                for i, slot in enumerate(some):
                    row = jnp.minimum(jnp.maximum(rows_ref[slot] - me * blocks, 0), blocks - 1)
                    x = by_block[g, row].astype(jnp.bfloat16)
                    lines.append(jnp.concatenate([zero, x] if i % 2 else [x, zero], axis=1))
                for i in range(0, len(some), 2):
                    pair = [tiles[slot] for slot in some[i : i + 2]]
                    if len(pair) == 1:
                        pair.append(jnp.zeros_like(pair[0]))
                    sides.append(jnp.concatenate(pair, axis=0))
                product = jnp.dot(
                    jnp.concatenate(lines, axis=0), jnp.concatenate(sides, axis=1),
                    preferred_element_type=jnp.float32,
                )
                for i, slot in enumerate(some):
                    both = product[8 * i : 8 * i + 8, i // 2 * 128 : i // 2 * 128 + 128]
                    sent[n, g, q, pl.ds(slot % CHUNK, half, stride=CHUNK), :] = (
                        both[:half] + both[half : 2 * half]
                    )
            if n == 0 and g == 0 and q == 0:
                sent[0, 0, 0, pl.ds(body, TARGET_ROWS), :] = own_ids
            copy = copy_of(n, g, q, sent.at[n], ACROSS, across)
            copy.start()
            started.append((None, copy))
        for q in range(chunks):
            near = copy_of(n, g, q, sent.at[n], PARTNER, partner)
            near.start()
            started.append((None, near))

    def grow(n):
        section = STEPS - 1 - n
        if n == 0:
            loads[3].wait()
        for first in range(0, levels, 8):
            rows = min(8, levels - first)
            part = pl.ds(first, rows)
            depth = lax.broadcasted_iota(jnp.int32, (rows, width), 0) + first
            light = jnp.exp(-0.2 * depth.astype(jnp.float32))
            c = [carried[t, part, :] for t in range(tracers)]
            bio = biology(c, [states[section, t, part, :] for t in range(tracers)], light)
            for t in range(tracers):
                adj[t, part, :] = c[t] + TIME_STEP * bio[t]

    def forward(n, g):
        for q in range(chunks):
            copy_of(n, g, q, sent.at[n], ACROSS, across).wait_recv()
            on = copy_of(n, g, q, got.at[n, ACROSS], RELAYED, relay_to)
            over = copy_of(n, g, q, got.at[n, ACROSS], PASSED, partner, pass_sem.at[n, g, q])
            pl.when(relays)(on.start)
            pl.when(passes)(over.start)
            started.extend([(relays, on), (passes, over)])

    def two(n, first, second):
        return jnp.where(
            lane < slots_pad,
            first[0, 0, pl.ds(body, TARGET_ROWS), :],
            second[0, 0, pl.ds(body, TARGET_ROWS), :],
        )

    def near(n, g):
        for q in range(chunks):
            copy_of(n, g, q, sent.at[n], PARTNER, partner).wait_recv()
        if "near" not in picks:
            ids = two(n, sent.at[0], got.at[0, PARTNER])
            ids = jnp.where(
                lane < 2 * slots_pad, ids, got[0, ACROSS, 0, 0, pl.ds(body, TARGET_ROWS), :]
            )
            picks["near"] = pick_of(ids[0:1, : 3 * slots_pad])
        total = placed(
            picks["near"], g, [sent.at[n], got.at[n, PARTNER], got.at[n, ACROSS]]
        )
        for i, t in enumerate(range(*groups[g])):
            adj[t] = adj[t] + total[:, i * 128 : (i + 1) * 128]

    def finish(n, g):
        for q in range(chunks):
            come = copy_of(n, g, q, got.at[n, ACROSS], RELAYED, relay_to)
            pl.when(relayed)(come.wait_recv)
            over = copy_of(n, g, q, got.at[n, RELAYED], PASSED, partner, pass_sem.at[n, g, q])
            pl.when(passes_relayed)(over.start)
            started.append((passes_relayed, over))
        for q in range(chunks):
            fourth = copy_of(n, g, q, got.at[n, ACROSS], PASSED, partner)
            pl.when(gets_fourth)(fourth.wait_recv)
        if "far" not in picks:
            ids = two(n, got.at[0, RELAYED], got.at[0, PASSED])
            picks["far"] = pick_of(ids[0:1, : 2 * slots_pad])
        total = placed(picks["far"], g, [got.at[n, RELAYED], got.at[n, PASSED]])
        mask = wet(0, levels)
        for i, t in enumerate(range(*groups[g])):
            late = total[:, i * 128 : (i + 1) * 128]
            if n == STEPS - 1:
                out_ref[t] = mask * (adj[t] + late)
            else:
                adj[t] = mask * (adj[t] + late)

    loads[0].wait()
    loads[1].wait()
    compute(0, 0)
    compute(0, 1)
    grow(0)
    for n in range(STEPS):
        forward(n, 0)
        near(n, 0)
        forward(n, 1)
        near(n, 1)
        finish(n, 0)
        if n < STEPS - 1:
            compute(n + 1, 0)
        finish(n, 1)
        if n < STEPS - 1:
            compute(n + 1, 1)
            grow(n + 1)
    for condition, copy in started:
        if condition is None:
            copy.wait_send()
        else:
            pl.when(condition)(copy.wait_send)


def shards(peers, final_adjoint, states, implicit, wet_levels, tile_rows, tile_cols, tiles, tile_count):
    tracers, levels, width = final_adjoint.shape
    blocks = levels * width // 128
    slots = tiles.shape[0]
    chunks = -(-slots // CHUNK)
    rows = tracer_groups(tracers)[0][1] * CHUNK + TARGET_ROWS
    hbm = pl.BlockSpec(memory_space=pl.ANY)
    smem = pl.BlockSpec(memory_space=pltpu.SMEM)
    vmem = pl.BlockSpec(memory_space=pltpu.VMEM)
    f32 = jnp.float32
    return pl.pallas_call(
        functools.partial(kernel, peers, slots, chunks, blocks),
        out_shape=jax.ShapeDtypeStruct((tracers, levels, width), f32),
        in_specs=[hbm, hbm, hbm, vmem, smem, smem, hbm, smem],
        out_specs=vmem,
        scratch_shapes=[
            pltpu.VMEM((tracers, levels, width), f32),
            pltpu.VMEM(states.shape, f32),
            pltpu.VMEM(implicit.shape, f32),
            pltpu.VMEM(tiles.shape, tiles.dtype),
            pltpu.VMEM((tracers, levels, width), f32),
            pltpu.VMEM((2, blocks, 8, 128), f32),
            pltpu.VMEM((STEPS, 2, chunks, rows, 128), f32),
            pltpu.VMEM((STEPS, 4, 2, chunks, rows, 128), f32),
            pltpu.SemaphoreType.DMA((4,)),
            pltpu.SemaphoreType.DMA((STEPS, 4, 2, chunks)),
            pltpu.SemaphoreType.DMA((STEPS, 4, 2, chunks)),
            pltpu.SemaphoreType.DMA((STEPS, 2, chunks)),
        ],
        compiler_params=pltpu.CompilerParams(
            collective_id=0, has_side_effects=True, vmem_limit_bytes=60 * 1024 * 1024
        ),
    )(
        final_adjoint, states, implicit, wet_levels.reshape(1, width),
        tile_rows, tile_cols, tiles, tile_count,
    )


def solution(mesh):
    in_specs = (
        P(None, None, "col"),
        P(None, None, None, "col"),
        P(None, None, "col"),
        P("col"),
        P("col"),
        P("col"),
        P("col", None, None),
        P("col"),
    )
    out_specs = P(None, None, "col")
    return jax.shard_map(
        functools.partial(shards, mesh.shape["col"]),
        mesh=mesh, in_specs=in_specs, out_specs=out_specs, check_vma=False,
    )
```
